512 devices in a mesh: dp: 64 (over x, y, core), tensor: 8 (over z).
Axes of the slice: x: 4, y: 8, z: 8, core: 2. Of those that a mesh axis runs over, the one named last changes fastest.
Arguments:
- queries: bfloat16 [8192, 4096], P('dp', 'tensor'), may hold values from -40 to 40
- keys: bfloat16 [106496, 1024], P(('dp', 'tensor')), may hold values from -40 to 40
- values: bfloat16 [106496, 1024], P(('dp', 'tensor')), may hold values from -6 to 6
- out_grad: bfloat16 [8192, 4096], P('dp', 'tensor'), may hold values from -6 to 6
- tile_counts: int32 [64], replicated, may hold values from 0 to 4, as said below
- text_sample: int32 [64], replicated, may hold values from 0 to 63, as said below
Outputs:
- query_grad: bfloat16 [8192, 4096], P('dp', 'tensor')
- key_grad: bfloat16 [106496, 1024], P(('dp', 'tensor'))
- value_grad: bfloat16 [106496, 1024], P(('dp', 'tensor'))
The draws below stay inside these ranges and needn't reach their ends.
Inputs may be any that keep to these rules, and one draw needn't show every extreme that they name: `tile_counts`: the counts of each aligned group of 4 samples sum to 4. `text_sample`: each sample once; index i holds a sample of its own aligned group of 4 indices.
All inputs are finite; a program needn't handle non-finite values.
Results may differ from the reference program's by a relative error of at most 0.011.
Values may be sent and summed in bfloat16 or wider, within the bound.
No kernel may reach another device: no remote copies, remote signals or barrier semaphores. Data moves between devices by JAX's collectives and lax.ppermute only.
A program may use at most 64 MiB of HBM per device.

```python
import jax
import jax.numpy as jnp
from jax import lax

Q_HEADS = 32
KV_HEADS = 8
HEAD_DIM = 128
TOK_DEV = 128
TILE_ROWS = 1601
TILE_PAD = 1664
TILE_DEV = 1
GROUP = 4
SAMPLES = 64
TEXT_ROWS = 8192
TILE_SLOTS = 64
N_DP = 64


def draw_queries(key, part):
    key = jax.random.fold_in(key, 11)
    per_kv = Q_HEADS // KV_HEADS
    base = jax.random.normal(key, (TEXT_ROWS, KV_HEADS, per_kv, HEAD_DIM), jnp.float32)
    return base.reshape(TEXT_ROWS, Q_HEADS * HEAD_DIM).astype(jnp.bfloat16)


def draw_keys(key, part):
    key = jax.random.fold_in(key, 12)
    base = jax.random.normal(key, (TILE_SLOTS * TILE_PAD, KV_HEADS, HEAD_DIM), jnp.float32)
    return base.reshape(TILE_SLOTS * TILE_PAD, KV_HEADS * HEAD_DIM).astype(jnp.bfloat16)


def draw_tile_counts(key, part):
    key = jax.random.fold_in(key, 13)
    groups = SAMPLES // GROUP
    tiles = GROUP * TILE_DEV
    assigned = jax.random.randint(key, (groups, tiles), 0, GROUP)
    assigned = assigned.at[0].set(0)
    members = jnp.arange(GROUP, dtype=jnp.int32)
    counts = jnp.sum((assigned[:, :, None] == members[None, None, :]).astype(jnp.int32), axis=1)
    return counts.reshape(SAMPLES).astype(jnp.int32)


def draw_text_sample(key, part):
    key = jax.random.fold_in(key, 17)
    groups = SAMPLES // GROUP
    row_keys = jax.random.split(key, groups)
    orders = jax.vmap(lambda row_key: jax.random.permutation(row_key, GROUP))(row_keys)
    orders = orders + jnp.arange(groups)[:, None] * GROUP
    return orders.reshape(SAMPLES).astype(jnp.int32)


def levels(stream_key, dims, shards, least, largest):
    gain = 1.0
    for position, shards_of in shards:
        draws = jax.random.uniform(jax.random.fold_in(jax.random.fold_in(stream_key, 6), position), (shards_of,), jnp.float32, least / len(shards), largest / len(shards))
        gain = gain * jnp.repeat(jnp.exp(draws), dims[position] // shards_of).reshape((-1,) + (1,) * (len(dims) - 1 - position))
    return gain


def gaussian(stream_key, dims, scale, limit, cuts=(), kind=jnp.bfloat16):
    array = jax.random.normal(stream_key, dims, jnp.float32) * scale
    if len(cuts) > 0:
        array = levels(stream_key, dims, cuts, -0.22, 0.18) * array
    return jnp.clip(array, min=-limit, max=limit).astype(kind)


def setup_inputs(seed: int = 0) -> dict:
    arg_keys = jax.random.split(jax.random.key(seed), 7)
    queries = draw_queries(jax.random.fold_in(arg_keys[6], 71), 0)
    keys = draw_keys(jax.random.fold_in(arg_keys[6], 71), 0)
    values = gaussian(arg_keys[2], (TILE_SLOTS * TILE_PAD, KV_HEADS * HEAD_DIM), 1.0, 6.0, ((0, 512),))
    out_grad = gaussian(arg_keys[3], (TEXT_ROWS, Q_HEADS * HEAD_DIM), 1.0, 6.0, ((0, 64), (1, 8)))
    tile_counts = draw_tile_counts(jax.random.fold_in(arg_keys[6], 71), 0)
    text_sample = draw_text_sample(jax.random.fold_in(arg_keys[6], 71), 0)
    return dict(queries=queries, keys=keys, values=values, out_grad=out_grad, tile_counts=tile_counts, text_sample=text_sample)


def slot_terms(query_rows, grad_rows, key_rows, value_rows):
    text_rows = query_rows.shape[0]
    kv_count = key_rows.shape[1] // HEAD_DIM
    per_kv = query_rows.shape[1] // HEAD_DIM // kv_count
    q_heads = query_rows.astype(jnp.float32).reshape(text_rows, kv_count, per_kv, HEAD_DIM)
    g_heads = grad_rows.astype(jnp.float32).reshape(text_rows, kv_count, per_kv, HEAD_DIM)
    k_heads = key_rows.astype(jnp.float32).reshape(key_rows.shape[0], kv_count, HEAD_DIM)
    v_heads = value_rows.astype(jnp.float32).reshape(key_rows.shape[0], kv_count, HEAD_DIM)
    scores = jnp.einsum('tkgd,rkd->kgtr', q_heads, k_heads) * (HEAD_DIM ** -0.5)
    live_rows = jnp.arange(key_rows.shape[0]) < TILE_ROWS
    scores = jnp.where(live_rows, scores, -1e30)
    grad_prod = jnp.einsum('tkgd,rkd->kgtr', g_heads, v_heads)
    return q_heads, g_heads, k_heads, v_heads, scores, grad_prod


def reference(queries, keys, values, out_grad, tile_counts, text_sample):
    softmax_scale = HEAD_DIM ** -0.5
    slot_ids = jnp.arange(TILE_SLOTS, dtype=jnp.int32)
    tile_ends = jnp.cumsum(tile_counts).astype(jnp.int32)
    slot_sample = jnp.sum((tile_ends[None, :] <= slot_ids[:, None]).astype(jnp.int32), axis=1)
    device_ids = jnp.arange(N_DP, dtype=jnp.int32)
    owner = jnp.sum(jnp.where(text_sample[None, :] == slot_sample[:, None], device_ids[None, :], 0), axis=1).astype(jnp.int32)

    def fetch(slot_index):
        start = (owner[slot_index] * TOK_DEV).astype(jnp.int32)
        key_start = (slot_index * TILE_PAD).astype(jnp.int32)
        query_rows = lax.dynamic_slice_in_dim(queries, start, TOK_DEV, 0)
        grad_rows = lax.dynamic_slice_in_dim(out_grad, start, TOK_DEV, 0)
        key_rows = lax.dynamic_slice_in_dim(keys, key_start, TILE_PAD, 0)
        value_rows = lax.dynamic_slice_in_dim(values, key_start, TILE_PAD, 0)
        return slot_terms(query_rows, grad_rows, key_rows, value_rows)

    def first_pass(slot_index):
        terms = fetch(slot_index)
        scores, grad_prod = terms[4], terms[5]
        maximum = jnp.max(scores, axis=-1)
        weights = jnp.exp(scores - maximum[..., None])
        return maximum, jnp.sum(weights, axis=-1), jnp.sum(weights * grad_prod, axis=-1)

    maxima, totals, products = lax.map(first_pass, slot_ids)
    top_value = jax.ops.segment_max(maxima, owner, num_segments=N_DP)
    rescale = jnp.exp(maxima - top_value[owner])
    total_sum = jax.ops.segment_sum(totals * rescale, owner, num_segments=N_DP)
    prod_sum = jax.ops.segment_sum(products * rescale, owner, num_segments=N_DP)
    safe_total = jnp.where(total_sum > 0, total_sum, 1.0)
    log_total = top_value + jnp.log(safe_total)
    row_delta = prod_sum / safe_total

    def second_pass(grad_acc, slot_index):
        q_heads, g_heads, k_heads, v_heads, scores, grad_prod = fetch(slot_index)
        holder = owner[slot_index]
        probs = jnp.exp(scores - log_total[holder][..., None])
        dscore = probs * (grad_prod - row_delta[holder][..., None])
        probs_low = lax.optimization_barrier(probs.astype(jnp.bfloat16)).astype(jnp.float32)
        dscore_low = lax.optimization_barrier(dscore.astype(jnp.bfloat16)).astype(jnp.float32)
        value_part = jnp.einsum('kgtr,tkgd->rkd', probs_low, g_heads)
        key_part = jnp.einsum('kgtr,tkgd->rkd', dscore_low, q_heads) * softmax_scale
        query_part = jnp.einsum('kgtr,rkd->tkgd', dscore_low, k_heads) * softmax_scale
        current = lax.dynamic_index_in_dim(grad_acc, holder, 0, keepdims=False)
        grad_acc = lax.dynamic_update_index_in_dim(grad_acc, current + query_part.reshape(TOK_DEV, -1), holder, 0)
        return grad_acc, (key_part.reshape(TILE_PAD, -1).astype(jnp.bfloat16), value_part.reshape(TILE_PAD, -1).astype(jnp.bfloat16))

    initial = jnp.zeros((N_DP, TOK_DEV, Q_HEADS * HEAD_DIM), jnp.float32)
    grad_acc, (key_parts, value_parts) = lax.scan(second_pass, initial, slot_ids)
    query_grad = grad_acc.reshape(N_DP * TOK_DEV, Q_HEADS * HEAD_DIM).astype(jnp.bfloat16)
    key_grad = key_parts.reshape(TILE_SLOTS * TILE_PAD, KV_HEADS * HEAD_DIM)
    value_grad = value_parts.reshape(TILE_SLOTS * TILE_PAD, KV_HEADS * HEAD_DIM)
    return query_grad, key_grad, value_grad
```

```python
import functools

import jax
import jax.numpy as jnp
from jax import lax
from jax.experimental import pallas as pl
from jax.experimental.pallas import tpu as pltpu
from jax.sharding import PartitionSpec as P

HEAD_DIM = 128
TILE_ROWS = 1601
GROUP = 4
SCALE = HEAD_DIM ** -0.5
LOG2E = 1.4426950408889634
SCALE2 = SCALE * LOG2E


def owners(dp, counts, text):
    first = (dp // GROUP) * GROUP
    end0 = counts[first]
    end1 = end0 + counts[first + 1]
    end2 = end1 + counts[first + 2]
    found = []
    for slot in range(GROUP):
        sample = first
        for end in (end0, end1, end2):
            sample = sample + jnp.where(end <= slot, 1, 0)
        owner = jnp.int32(0)
        for member in range(1, GROUP):
            owner = owner + jnp.where(text[first + member] == sample, member, 0)
        found.append(owner)
    return found, dp - first


def pick(options, position):
    chosen = options[0]
    for index in range(1, GROUP):
        chosen = jnp.where(position == index, options[index], chosen)
    return chosen


def head_rows(block):
    heads = block.shape[1] // HEAD_DIM
    return jnp.concatenate([block[:, h * HEAD_DIM:(h + 1) * HEAD_DIM] for h in range(heads)], axis=0)


def scores_of(kv_ref, part, q_rows):
    rows = kv_ref.shape[2]
    scores = lax.dot_general(
        kv_ref[part, 0], q_rows, (((1,), (1,)), ((), ())), preferred_element_type=jnp.float32
    ) * SCALE2
    if (part + 1) * rows > TILE_ROWS:
        row = lax.broadcasted_iota(jnp.int32, scores.shape, 0) + part * rows
        scores = jnp.where(row < TILE_ROWS, scores, -1e30)
    return scores


def grad_of(kv_ref, part, g_rows):
    return lax.dot_general(
        kv_ref[part, 1], g_rows, (((1,), (1,)), ((), ())), preferred_element_type=jnp.float32
    )


def stats_kernel(dp_ref, counts_ref, text_ref, q_ref, g_ref, kv_ref, stat_ref, score_ref):
    found, position = owners(dp_ref[0], counts_ref, text_ref)
    mine = pick(found, position)
    q_rows = head_rows(q_ref[mine])
    g_rows = head_rows(g_ref[mine])
    parts, rows = kv_ref.shape[0], kv_ref.shape[2]
    top = None
    for part in range(parts):
        scores = scores_of(kv_ref, part, q_rows)
        score_ref[pl.ds(part * rows, rows), :] = scores
        part_top = jnp.max(scores, axis=0, keepdims=True)
        top = part_top if top is None else jnp.maximum(top, part_top)
    total = jnp.zeros_like(top)
    product = jnp.zeros_like(top)
    for part in range(parts):
        weights = jnp.exp2(score_ref[pl.ds(part * rows, rows), :] - top)
        total = total + jnp.sum(weights, axis=0, keepdims=True)
        product = product + jnp.sum(weights * grad_of(kv_ref, part, g_rows), axis=0, keepdims=True)
    stat_ref[...] = jnp.concatenate([top, total, product, jnp.zeros((5, top.shape[1]), jnp.float32)], axis=0)


def grads_kernel(dp_ref, counts_ref, text_ref, stat_ref, q_ref, g_ref, kv_ref, out_ref, dq_ref):
    found, position = owners(dp_ref[0], counts_ref, text_ref)
    mine = pick(found, position)
    q_rows = head_rows(q_ref[mine])
    g_rows = head_rows(g_ref[mine])
    stats = []
    top = None
    for slot in range(GROUP):
        same = found[slot] == mine
        block = stat_ref[slot]
        slot_top = jnp.where(same, block[0:1], -1e30)
        stats.append((same, slot_top, block[1:2], block[2:3]))
        top = slot_top if top is None else jnp.maximum(top, slot_top)
    total = jnp.zeros_like(top)
    product = jnp.zeros_like(top)
    for same, slot_top, slot_total, slot_product in stats:
        weight = jnp.where(same, jnp.exp2(slot_top - top), 0.0)
        total = total + weight * slot_total
        product = product + weight * slot_product
    log_total = top + jnp.log2(total)
    delta = product / total
    parts = kv_ref.shape[0]
    dq = None
    for part in range(parts):
        probs = jnp.exp2(scores_of(kv_ref, part, q_rows) - log_total)
        dscore = probs * (grad_of(kv_ref, part, g_rows) - delta)
        probs = probs.astype(jnp.bfloat16)
        dscore = dscore.astype(jnp.bfloat16)
        value_part = jnp.dot(probs, g_rows, preferred_element_type=jnp.float32)
        key_part = jnp.dot(dscore, q_rows, preferred_element_type=jnp.float32) * SCALE
        out_ref[part, 0] = key_part.astype(jnp.bfloat16)
        out_ref[part, 1] = value_part.astype(jnp.bfloat16)
        query_part = lax.dot_general(
            kv_ref[part, 0], dscore, (((0,), (0,)), ((), ())), preferred_element_type=jnp.float32
        )
        dq = query_part if dq is None else dq + query_part
    for head in range(dq.shape[1] // HEAD_DIM):
        cols = slice(head * HEAD_DIM, (head + 1) * HEAD_DIM)
        dq_ref[:, cols] = (dq[:, cols].T * SCALE).astype(jnp.bfloat16)


def query_kernel(dp_ref, counts_ref, text_ref, parts_ref, out_ref):
    found, position = owners(dp_ref[0], counts_ref, text_ref)
    total = jnp.zeros(out_ref.shape, jnp.float32)
    for slot in range(GROUP):
        total = total + jnp.where(found[slot] == position, parts_ref[slot].astype(jnp.float32), 0.0)
    out_ref[...] = total.astype(jnp.bfloat16)


SMEM = pl.BlockSpec(memory_space=pltpu.SMEM)
VMEM = pl.BlockSpec(memory_space=pltpu.VMEM)


def call(kernel, out_shape, scalars, arrays, scratch=(), flops=0, exps=0):
    outs = out_shape if isinstance(out_shape, tuple) else (out_shape,)
    moved = sum(a.size * a.dtype.itemsize for a in arrays) + sum(o.size * o.dtype.itemsize for o in outs)
    return pl.pallas_call(
        kernel,
        out_shape=out_shape,
        in_specs=[SMEM] * len(scalars) + [VMEM] * len(arrays),
        out_specs=tuple(VMEM for _ in outs) if isinstance(out_shape, tuple) else VMEM,
        scratch_shapes=scratch,
        compiler_params=pltpu.CompilerParams(vmem_limit_bytes=32 * 1024 * 1024),
        cost_estimate=pl.CostEstimate(flops=flops, bytes_accessed=moved, transcendentals=exps),
    )(*scalars, *arrays)


def on_device(queries, keys, values, out_grad, tile_counts, text_sample):
    text_rows, width = queries.shape
    rows = keys.shape[0]
    parts = lax.axis_size("tensor")
    devices = lax.axis_size("dp")
    groups = [[first + member for member in range(GROUP)] for first in range(0, devices, GROUP)]
    gather = functools.partial(lax.all_gather, axis_name="dp", axis_index_groups=groups)
    scalars = (lax.axis_index("dp").astype(jnp.int32).reshape(1), tile_counts, text_sample)
    heads = text_rows * width // HEAD_DIM
    matmul = 2 * heads * parts * rows * HEAD_DIM

    packed = jnp.stack([keys.reshape(rows, parts, HEAD_DIM), values.reshape(rows, parts, HEAD_DIM)])
    kv = lax.all_to_all(packed.transpose(2, 0, 1, 3), "tensor", 0, 0, tiled=True)
    q_all = gather(queries)
    g_all = gather(out_grad)
    stats = call(
        stats_kernel,
        jax.ShapeDtypeStruct((8, heads), jnp.float32),
        scalars,
        (q_all, g_all, kv),
        scratch=[pltpu.VMEM((parts * rows, heads), jnp.float32)],
        flops=2 * matmul,
        exps=heads * parts * rows,
    )
    stats_all = gather(stats)
    grads, dq = call(
        grads_kernel,
        (
            jax.ShapeDtypeStruct((parts, 2, rows, HEAD_DIM), jnp.bfloat16),
            jax.ShapeDtypeStruct((text_rows, width), jnp.bfloat16),
        ),
        scalars,
        (stats_all, q_all, g_all, kv),
        flops=5 * matmul,
        exps=heads * parts * rows,
    )
    back = lax.all_to_all(grads, "tensor", 0, 0, tiled=True)
    dq_all = gather(dq)
    query_grad = call(query_kernel, jax.ShapeDtypeStruct((text_rows, width), jnp.bfloat16), scalars, (dq_all,))
    back = back.transpose(1, 2, 0, 3).reshape(2, rows, parts * HEAD_DIM)
    return query_grad, back[0], back[1]


def solution(mesh):
    return jax.shard_map(
        on_device,
        mesh=mesh,
        in_specs=(
            P("dp", "tensor"),
            P(("dp", "tensor"), None),
            P(("dp", "tensor"), None),
            P("dp", "tensor"),
            P(),
            P(),
        ),
        out_specs=(P("dp", "tensor"), P(("dp", "tensor"), None), P(("dp", "tensor"), None)),
        check_vma=False,
    )
```

```python
import functools
import math

import jax
import jax.numpy as jnp
from jax import lax
from jax.experimental import pallas as pl
from jax.experimental.pallas import tpu as pltpu
from jax.sharding import PartitionSpec as P

HEAD_DIM = 128
TILE_ROWS = 1601
GROUP = 4
SCALE = HEAD_DIM ** -0.5
LOG2E = 1.4426950408889634
SCALE2 = SCALE * LOG2E


def owners(dp, counts, text):
    first = (dp // GROUP) * GROUP
    end0 = counts[first]
    end1 = end0 + counts[first + 1]
    end2 = end1 + counts[first + 2]
    found = []
    for slot in range(GROUP):
        sample = first
        for end in (end0, end1, end2):
            sample = sample + jnp.where(end <= slot, 1, 0)
        owner = jnp.int32(0)
        for member in range(1, GROUP):
            owner = owner + jnp.where(text[first + member] == sample, member, 0)
        found.append(owner)
    return found, dp - first


def pick(options, position):
    chosen = options[0]
    for index in range(1, GROUP):
        chosen = jnp.where(position == index, options[index], chosen)
    return chosen


def head_rows(block):
    heads = block.shape[1] // HEAD_DIM
    return jnp.concatenate([block[:, h * HEAD_DIM:(h + 1) * HEAD_DIM] for h in range(heads)], axis=0)


def member_order(size):
    return [(size - 1 + index) % size for index in range(size)]


def pack_kernel(order, keys_ref, values_ref, out_ref, held, in_sems, out_sems):
    parts = out_ref.shape[0]
    loads = []
    for part in range(parts):
        for side, ref in enumerate((keys_ref, values_ref)):
            columns = ref.at[:, pl.ds(order[part] * HEAD_DIM, HEAD_DIM)]
            loads.append(pltpu.make_async_copy(columns, held.at[part, side], in_sems.at[part, side]))
            loads[-1].start()
    stores = []
    for part in range(parts):
        loads[2 * part].wait()
        loads[2 * part + 1].wait()
        stores.append(pltpu.make_async_copy(held.at[part], out_ref.at[part], out_sems.at[part]))
        stores[-1].start()
    for store in stores:
        store.wait()


def unpack_kernel(order, in_ref, keys_ref, values_ref, sems):
    copies = []
    for side, ref in enumerate((keys_ref, values_ref)):
        for part in range(in_ref.shape[0]):
            columns = ref.at[:, pl.ds(order[part] * HEAD_DIM, HEAD_DIM)]
            copies.append(pltpu.make_async_copy(in_ref.at[part, side], columns, sems.at[part, side]))
    for copy in copies:
        copy.start()
    for copy in copies:
        copy.wait()


def text_kernel(dp_ref, counts_ref, text_ref, q_ref, g_ref, flag_ref, qt_ref, gt_ref, q_out_ref, g_out_ref):
    found, position = owners(dp_ref[0], counts_ref, text_ref)
    mine = pick(found, position)
    for ref, out_ref, turned_ref in ((q_ref, q_out_ref, qt_ref), (g_ref, g_out_ref, gt_ref)):
        rows = head_rows(ref[mine])
        out_ref[...] = rows
        turned_ref[...] = rows.T
    for slot in range(GROUP):
        line = jnp.zeros((1, flag_ref.shape[1]), jnp.float32)
        flag_ref[slot:slot + 1] = line + jnp.where(found[slot] == mine, 1.0, 0.0)
        flag_ref[GROUP + slot:GROUP + slot + 1] = line + jnp.where(found[slot] == position, 1.0, 0.0)


def stats_kernel(order, qt_ref, gt_ref, kv_ref, stat_ref, weight_ref, grad_ref):
    parts, rows = kv_ref.shape[0], kv_ref.shape[2]
    q_turned, g_turned = qt_ref[...], gt_ref[...]
    top = None
    for part in range(parts):
        scores = jnp.dot(kv_ref[part, 0], q_turned, preferred_element_type=jnp.float32) * SCALE2
        if (order[part] + 1) * rows > TILE_ROWS:
            row = lax.broadcasted_iota(jnp.int32, scores.shape, 0) + order[part] * rows
            scores = jnp.where(row < TILE_ROWS, scores, -1e30)
        weight_ref[pl.ds(part * rows, rows), :] = scores
        part_top = jnp.max(scores, axis=0, keepdims=True)
        top = part_top if top is None else jnp.maximum(top, part_top)
    total = jnp.zeros_like(top)
    product = jnp.zeros_like(top)
    for part in range(parts):
        span = pl.ds(part * rows, rows)
        weights = jnp.exp2(weight_ref[span, :] - top)
        weight_ref[span, :] = weights
        grads = jnp.dot(kv_ref[part, 1], g_turned, preferred_element_type=jnp.float32)
        grad_ref[span, :] = grads
        total = total + jnp.sum(weights, axis=0, keepdims=True)
        product = product + jnp.sum(weights * grads, axis=0, keepdims=True)
    stat_ref[...] = jnp.concatenate([top, total, product, jnp.zeros((5, top.shape[1]), jnp.float32)], axis=0)


def grads_kernel(
    flag_ref, all_ref, own_ref, q_ref, g_ref, kv_ref, weight_ref, grad_ref, out_ref, dq_ref, held, sems
):
    tops = [jnp.where(flag_ref[slot:slot + 1] > 0, all_ref[slot][0:1], -1e30) for slot in range(GROUP)]
    top = functools.reduce(jnp.maximum, tops)
    total = jnp.zeros_like(top)
    product = jnp.zeros_like(top)
    for slot in range(GROUP):
        share = jnp.where(flag_ref[slot:slot + 1] > 0, jnp.exp2(tops[slot] - top), 0.0)
        total = total + share * all_ref[slot][1:2]
        product = product + share * all_ref[slot][2:3]
    delta = product / total
    rescale = jnp.exp2(own_ref[0:1] - top) / total
    parts, rows = kv_ref.shape[0], kv_ref.shape[2]
    q_rows, g_rows = q_ref[...], g_ref[...]
    dq = None
    copies = []
    for part in range(parts):
        span = pl.ds(part * rows, rows)
        probs = weight_ref[span, :] * rescale
        dscore = (probs * (grad_ref[span, :] - delta)).astype(jnp.bfloat16)
        probs = probs.astype(jnp.bfloat16)
        held[part, 0] = (jnp.dot(dscore, q_rows, preferred_element_type=jnp.float32) * SCALE).astype(jnp.bfloat16)
        held[part, 1] = jnp.dot(probs, g_rows, preferred_element_type=jnp.float32).astype(jnp.bfloat16)
        copies.append(pltpu.make_async_copy(held.at[part], out_ref.at[part], sems.at[part]))
        copies[-1].start()
        query_part = lax.dot_general(
            kv_ref[part, 0], dscore, (((0,), (0,)), ((), ())), preferred_element_type=jnp.float32
        )
        dq = query_part if dq is None else dq + query_part
    for head in range(dq.shape[1] // HEAD_DIM):
        cols = slice(head * HEAD_DIM, (head + 1) * HEAD_DIM)
        dq_ref[:, cols] = (dq[:, cols].T * SCALE).astype(jnp.bfloat16)
    for copy in copies:
        copy.wait()


def query_kernel(flag_ref, parts_ref, out_ref):
    total = jnp.zeros(out_ref.shape, jnp.float32)
    for slot in range(GROUP):
        flag = flag_ref[GROUP + slot:GROUP + slot + 1]
        total = total + jnp.where(flag > 0, parts_ref[slot].astype(jnp.float32), 0.0)
    out_ref[...] = total.astype(jnp.bfloat16)


SMEM = pl.BlockSpec(memory_space=pltpu.SMEM)
VMEM = pl.BlockSpec(memory_space=pltpu.VMEM)
ANY = pl.BlockSpec(memory_space=pl.ANY)
MIB = 1024 * 1024


def call(kernel, out_shape, out_specs, in_specs, args, scratch=(), limit=32, flops=0, exps=0):
    outs = out_shape if isinstance(out_shape, tuple) else (out_shape,)
    moved = sum(a.size * a.dtype.itemsize for a in args) + sum(math.prod(o.shape) * 2 for o in outs)
    return pl.pallas_call(
        kernel,
        out_shape=out_shape,
        in_specs=in_specs,
        out_specs=out_specs,
        scratch_shapes=scratch,
        compiler_params=pltpu.CompilerParams(vmem_limit_bytes=limit * MIB),
        cost_estimate=pl.CostEstimate(flops=flops, bytes_accessed=moved, transcendentals=exps),
    )(*args)


def on_device(queries, keys, values, out_grad, tile_counts, text_sample):
    text_rows, width = queries.shape
    rows = keys.shape[0]
    parts = lax.axis_size("tensor")
    order = member_order(parts)
    exchange = functools.partial(
        lax.all_to_all, axis_name="tensor", split_axis=0, concat_axis=0, axis_index_groups=[order], tiled=True
    )
    devices = lax.axis_size("dp")
    groups = [[first + member for member in range(GROUP)] for first in range(0, devices, GROUP)]
    gather = functools.partial(lax.all_gather, axis_name="dp", axis_index_groups=groups)
    position = lax.axis_index("dp").astype(jnp.int32).reshape(1)
    heads = text_rows * width // HEAD_DIM
    matmul = 2 * heads * parts * rows * HEAD_DIM
    half = jnp.bfloat16
    full = jnp.float32
    blocks = (parts, 2, rows, HEAD_DIM)

    packed = call(
        functools.partial(pack_kernel, order),
        jax.ShapeDtypeStruct(blocks, half),
        ANY,
        [ANY, ANY],
        (keys, values),
        scratch=[
            pltpu.VMEM(blocks, half),
            pltpu.SemaphoreType.DMA((parts, 2)),
            pltpu.SemaphoreType.DMA((parts,)),
        ],
        limit=60,
    )
    kv = exchange(packed)
    q_all = gather(queries)
    g_all = gather(out_grad)
    flags, q_turned, g_turned, q_rows, g_rows = call(
        text_kernel,
        (
            pltpu.VMEM((2 * GROUP, heads), full),
            pltpu.VMEM((HEAD_DIM, heads), half),
            pltpu.VMEM((HEAD_DIM, heads), half),
            pltpu.VMEM((heads, HEAD_DIM), half),
            pltpu.VMEM((heads, HEAD_DIM), half),
        ),
        (VMEM,) * 5,
        [SMEM] * 3 + [VMEM] * 2,
        (position, tile_counts, text_sample, q_all, g_all),
    )
    stats, weights, grad_prod = call(
        functools.partial(stats_kernel, order),
        (
            pltpu.VMEM((8, heads), full),
            pltpu.VMEM((parts * rows, heads), full),
            pltpu.VMEM((parts * rows, heads), full),
        ),
        (VMEM,) * 3,
        [VMEM] * 3,
        (q_turned, g_turned, kv),
        flops=2 * matmul,
        exps=heads * parts * rows,
    )
    stats_all = gather(stats)
    grads, dq = call(
        grads_kernel,
        (jax.ShapeDtypeStruct(blocks, half), pltpu.VMEM((text_rows, width), half)),
        (ANY, VMEM),
        [VMEM] * 8,
        (flags, stats_all, stats, q_rows, g_rows, kv, weights, grad_prod),
        scratch=[pltpu.VMEM(blocks, half), pltpu.SemaphoreType.DMA((parts,))],
        flops=3 * matmul,
    )
    back = exchange(grads)
    dq_all = gather(dq)
    query_grad = call(
        query_kernel, jax.ShapeDtypeStruct((text_rows, width), half), VMEM, [VMEM] * 2, (flags, dq_all)
    )
    tile = jax.ShapeDtypeStruct((rows, parts * HEAD_DIM), half)
    key_grad, value_grad = call(
        functools.partial(unpack_kernel, order),
        (tile, tile),
        (ANY, ANY),
        [ANY],
        (back,),
        scratch=[pltpu.SemaphoreType.DMA((parts, 2))],
        limit=8,
    )
    return query_grad, key_grad, value_grad


def solution(mesh):
    return jax.shard_map(
        on_device,
        mesh=mesh,
        in_specs=(
            P("dp", "tensor"),
            P(("dp", "tensor"), None),
            P(("dp", "tensor"), None),
            P("dp", "tensor"),
            P(),
            P(),
        ),
        out_specs=(P("dp", "tensor"), P(("dp", "tensor"), None), P(("dp", "tensor"), None)),
        check_vma=False,
    )
```

```python
import functools
import math

import jax
import jax.numpy as jnp
from jax import lax
from jax.experimental import pallas as pl
from jax.experimental.pallas import tpu as pltpu
from jax.sharding import PartitionSpec as P

HEAD_DIM = 128
TILE_ROWS = 1601
GROUP = 4
SCALE = HEAD_DIM ** -0.5
LOG2E = 1.4426950408889634
SCALE2 = SCALE * LOG2E


def owners(dp, counts, text):
    first = (dp // GROUP) * GROUP
    end0 = counts[first]
    end1 = end0 + counts[first + 1]
    end2 = end1 + counts[first + 2]
    found = []
    for slot in range(GROUP):
        sample = first
        for end in (end0, end1, end2):
            sample = sample + jnp.where(end <= slot, 1, 0)
        owner = jnp.int32(0)
        for member in range(1, GROUP):
            owner = owner + jnp.where(text[first + member] == sample, member, 0)
        found.append(owner)
    return found, dp - first


def pick(options, position):
    chosen = options[0]
    for index in range(1, GROUP):
        chosen = jnp.where(position == index, options[index], chosen)
    return chosen


def head_rows(block):
    heads = block.shape[1] // HEAD_DIM
    return jnp.concatenate([block[:, h * HEAD_DIM:(h + 1) * HEAD_DIM] for h in range(heads)], axis=0)


def member_order(first, size):
    return [(first + index) % size for index in range(size)]


def pack_kernel(order, keys_ref, values_ref, out_ref, held, in_sems, out_sems):
    parts = out_ref.shape[0]
    loads = []
    for part in range(parts):
        for side, ref in enumerate((keys_ref, values_ref)):
            columns = ref.at[:, pl.ds(order[part] * HEAD_DIM, HEAD_DIM)]
            loads.append(pltpu.make_async_copy(columns, held.at[part, side], in_sems.at[part, side]))
            loads[-1].start()
    stores = []
    for part in range(parts):
        loads[2 * part].wait()
        loads[2 * part + 1].wait()
        stores.append(pltpu.make_async_copy(held.at[part], out_ref.at[part], out_sems.at[part]))
        stores[-1].start()
    for store in stores:
        store.wait()


def unpack_kernel(order, in_ref, keys_ref, values_ref, sems):
    copies = []
    for side, ref in enumerate((keys_ref, values_ref)):
        for part in range(in_ref.shape[0]):
            columns = ref.at[:, pl.ds(order[part] * HEAD_DIM, HEAD_DIM)]
            copies.append(pltpu.make_async_copy(in_ref.at[part, side], columns, sems.at[part, side]))
    for copy in copies:
        copy.start()
    for copy in copies:
        copy.wait()


def text_kernel(dp_ref, counts_ref, text_ref, q_ref, g_ref, flag_ref, qt_ref, gt_ref, q_out_ref, g_out_ref):
    found, position = owners(dp_ref[0], counts_ref, text_ref)
    mine = pick(found, position)
    for ref, out_ref, turned_ref in ((q_ref, q_out_ref, qt_ref), (g_ref, g_out_ref, gt_ref)):
        rows = head_rows(ref[mine])
        out_ref[...] = rows
        turned_ref[...] = rows.T
    for slot in range(GROUP):
        line = jnp.zeros((1, flag_ref.shape[1]), jnp.float32)
        flag_ref[slot:slot + 1] = line + jnp.where(found[slot] == mine, 1.0, 0.0)
        flag_ref[GROUP + slot:GROUP + slot + 1] = line + jnp.where(found[slot] == position, 1.0, 0.0)


def stats_kernel(order, qt_ref, gt_ref, kv_ref, stat_ref, weight_ref, grad_ref):
    parts, rows = kv_ref.shape[0], kv_ref.shape[2]
    q_turned, g_turned = qt_ref[...], gt_ref[...]
    top = None
    for part in range(parts):
        scores = jnp.dot(kv_ref[part, 0], q_turned, preferred_element_type=jnp.float32) * SCALE2
        if (order[part] + 1) * rows > TILE_ROWS:
            row = lax.broadcasted_iota(jnp.int32, scores.shape, 0) + order[part] * rows
            scores = jnp.where(row < TILE_ROWS, scores, -1e30)
        weight_ref[pl.ds(part * rows, rows), :] = scores
        part_top = jnp.max(scores, axis=0, keepdims=True)
        top = part_top if top is None else jnp.maximum(top, part_top)
    total = jnp.zeros_like(top)
    product = jnp.zeros_like(top)
    for part in range(parts):
        span = pl.ds(part * rows, rows)
        weights = jnp.exp2(weight_ref[span, :] - top)
        weight_ref[span, :] = weights
        grads = jnp.dot(kv_ref[part, 1], g_turned, preferred_element_type=jnp.float32)
        grad_ref[span, :] = grads
        total = total + jnp.sum(weights, axis=0, keepdims=True)
        product = product + jnp.sum(weights * grads, axis=0, keepdims=True)
    stat_ref[...] = jnp.concatenate([top, total, product, jnp.zeros((5, top.shape[1]), jnp.float32)], axis=0)


def merged(flag_ref, all_ref):
    tops = [jnp.where(flag_ref[slot:slot + 1] > 0, all_ref[slot][0:1], -1e30) for slot in range(GROUP)]
    top = functools.reduce(jnp.maximum, tops)
    total = jnp.zeros_like(top)
    product = jnp.zeros_like(top)
    for slot in range(GROUP):
        share = jnp.where(flag_ref[slot:slot + 1] > 0, jnp.exp2(tops[slot] - top), 0.0)
        total = total + share * all_ref[slot][1:2]
        product = product + share * all_ref[slot][2:3]
    return top, 1.0 / total, product / total


def grads_kernel(
    places, flag_ref, all_ref, own_ref, q_ref, g_ref, weight_ref, grad_ref, out_ref, dscore_ref, held, sems
):
    top, inverse, delta = merged(flag_ref, all_ref)
    rescale = jnp.exp2(own_ref[0:1] - top) * inverse
    parts, rows = out_ref.shape[0], out_ref.shape[2]
    q_rows, g_rows = q_ref[...], g_ref[...]
    copies = []
    for part in range(parts):
        span = pl.ds(part * rows, rows)
        probs = weight_ref[span, :] * rescale
        dscore = (probs * (grad_ref[span, :] - delta)).astype(jnp.bfloat16)
        dscore_ref[span, :] = dscore
        probs = probs.astype(jnp.bfloat16)
        place = places[part]
        held[place, 0] = (jnp.dot(dscore, q_rows, preferred_element_type=jnp.float32) * SCALE).astype(jnp.bfloat16)
        held[place, 1] = jnp.dot(probs, g_rows, preferred_element_type=jnp.float32).astype(jnp.bfloat16)
        copies.append(pltpu.make_async_copy(held.at[place], out_ref.at[place], sems.at[part]))
        copies[-1].start()
    for copy in copies:
        copy.wait()


def text_grad_kernel(kv_ref, dscore_ref, dq_ref):
    parts, rows = kv_ref.shape[0], kv_ref.shape[2]
    dq = None
    for part in range(parts):
        query_part = lax.dot_general(
            kv_ref[part, 0],
            dscore_ref[pl.ds(part * rows, rows), :],
            (((0,), (0,)), ((), ())),
            preferred_element_type=jnp.float32,
        )
        dq = query_part if dq is None else dq + query_part
    for head in range(dq.shape[1] // HEAD_DIM):
        cols = slice(head * HEAD_DIM, (head + 1) * HEAD_DIM)
        dq_ref[:, cols] = (dq[:, cols].T * SCALE).astype(jnp.bfloat16)


def query_kernel(flag_ref, parts_ref, out_ref):
    total = jnp.zeros(out_ref.shape, jnp.float32)
    for slot in range(GROUP):
        flag = flag_ref[GROUP + slot:GROUP + slot + 1]
        total = total + jnp.where(flag > 0, parts_ref[slot].astype(jnp.float32), 0.0)
    out_ref[...] = total.astype(jnp.bfloat16)


SMEM = pl.BlockSpec(memory_space=pltpu.SMEM)
VMEM = pl.BlockSpec(memory_space=pltpu.VMEM)
HBM = pl.BlockSpec(memory_space=pltpu.HBM)
ANY = pl.BlockSpec(memory_space=pl.ANY)
MIB = 1024 * 1024


def call(kernel, out_shape, out_specs, in_specs, args, scratch=(), limit=32, flops=0, exps=0):
    outs = out_shape if isinstance(out_shape, tuple) else (out_shape,)
    moved = sum(a.size * a.dtype.itemsize for a in args) + sum(math.prod(o.shape) * 2 for o in outs)
    return pl.pallas_call(
        kernel,
        out_shape=out_shape,
        in_specs=in_specs,
        out_specs=out_specs,
        scratch_shapes=scratch,
        compiler_params=pltpu.CompilerParams(vmem_limit_bytes=limit * MIB),
        cost_estimate=pl.CostEstimate(flops=flops, bytes_accessed=moved, transcendentals=exps),
    )(*args)


def on_device(queries, keys, values, out_grad, tile_counts, text_sample):
    text_rows, width = queries.shape
    rows = keys.shape[0]
    parts = lax.axis_size("tensor")
    order = member_order(parts - 2, parts)
    back_order = member_order(parts - 3, parts)
    exchange = functools.partial(lax.all_to_all, axis_name="tensor", split_axis=0, concat_axis=0, tiled=True)
    devices = lax.axis_size("dp")
    groups = [[first + member for member in range(GROUP)] for first in range(0, devices, GROUP)]
    gather = functools.partial(lax.all_gather, axis_name="dp", axis_index_groups=groups)
    position = lax.axis_index("dp").astype(jnp.int32).reshape(1)
    heads = text_rows * width // HEAD_DIM
    matmul = 2 * heads * parts * rows * HEAD_DIM
    half = jnp.bfloat16
    full = jnp.float32
    blocks = (parts, 2, rows, HEAD_DIM)

    packed = call(
        functools.partial(pack_kernel, order),
        pltpu.HBM(blocks, half),
        HBM,
        [ANY, ANY],
        (keys, values),
        scratch=[
            pltpu.VMEM(blocks, half),
            pltpu.SemaphoreType.DMA((parts, 2)),
            pltpu.SemaphoreType.DMA((parts,)),
        ],
        limit=60,
    )
    kv = exchange(packed, axis_index_groups=[order])
    q_all = gather(queries)
    g_all = gather(out_grad)
    flags, q_turned, g_turned, q_rows, g_rows = call(
        text_kernel,
        (
            pltpu.VMEM((2 * GROUP, heads), full),
            pltpu.VMEM((HEAD_DIM, heads), half),
            pltpu.VMEM((HEAD_DIM, heads), half),
            pltpu.VMEM((heads, HEAD_DIM), half),
            pltpu.VMEM((heads, HEAD_DIM), half),
        ),
        (VMEM,) * 5,
        [SMEM] * 3 + [VMEM] * 2,
        (position, tile_counts, text_sample, q_all, g_all),
    )
    stats, weights, grad_prod = call(
        functools.partial(stats_kernel, order),
        (
            pltpu.VMEM((8, heads), full),
            pltpu.VMEM((parts * rows, heads), full),
            pltpu.VMEM((parts * rows, heads), full),
        ),
        (VMEM,) * 3,
        [VMEM] * 3,
        (q_turned, g_turned, kv),
        flops=2 * matmul,
        exps=heads * parts * rows,
    )
    stats_all = gather(stats)
    grads, dscore = call(
        functools.partial(grads_kernel, [back_order.index(member) for member in order]),
        (pltpu.HBM(blocks, half), pltpu.VMEM((parts * rows, heads), half)),
        (HBM, VMEM),
        [VMEM] * 7,
        (flags, stats_all, stats, q_rows, g_rows, weights, grad_prod),
        scratch=[pltpu.VMEM(blocks, half), pltpu.SemaphoreType.DMA((parts,))],
        flops=2 * matmul,
    )
    back = exchange(grads, axis_index_groups=[back_order])
    dq = call(
        text_grad_kernel,
        pltpu.VMEM((text_rows, width), half),
        VMEM,
        [VMEM] * 2,
        (kv, dscore),
        flops=matmul,
    )
    dq_all = gather(dq)
    query_grad = call(
        query_kernel, jax.ShapeDtypeStruct((text_rows, width), half), VMEM, [VMEM] * 2, (flags, dq_all)
    )
    tile = jax.ShapeDtypeStruct((rows, parts * HEAD_DIM), half)
    key_grad, value_grad = call(
        functools.partial(unpack_kernel, back_order),
        (tile, tile),
        (ANY, ANY),
        [ANY],
        (back,),
        scratch=[pltpu.SemaphoreType.DMA((parts, 2))],
        limit=8,
    )
    return query_grad, key_grad, value_grad


def solution(mesh):
    return jax.shard_map(
        on_device,
        mesh=mesh,
        in_specs=(
            P("dp", "tensor"),
            P(("dp", "tensor"), None),
            P(("dp", "tensor"), None),
            P("dp", "tensor"),
            P(),
            P(),
        ),
        out_specs=(P("dp", "tensor"), P(("dp", "tensor"), None), P(("dp", "tensor"), None)),
        check_vma=False,
    )
```

```python
import functools
import math

import jax
import jax.numpy as jnp
from jax import lax
from jax.experimental import pallas as pl
from jax.experimental.pallas import tpu as pltpu
from jax.sharding import PartitionSpec as P

HEAD_DIM = 128
TILE_ROWS = 1601
GROUP = 4
SCALE = HEAD_DIM ** -0.5
LOG2E = 1.4426950408889634
SCALE2 = SCALE * LOG2E


def owners(dp, counts, text):
    first = (dp // GROUP) * GROUP
    end0 = counts[first]
    end1 = end0 + counts[first + 1]
    end2 = end1 + counts[first + 2]
    found = []
    for slot in range(GROUP):
        sample = first
        for end in (end0, end1, end2):
            sample = sample + jnp.where(end <= slot, 1, 0)
        owner = jnp.int32(0)
        for member in range(1, GROUP):
            owner = owner + jnp.where(text[first + member] == sample, member, 0)
        found.append(owner)
    return found, dp - first


def pick(options, position):
    chosen = options[0]
    for index in range(1, GROUP):
        chosen = jnp.where(position == index, options[index], chosen)
    return chosen


def head_rows(block):
    heads = block.shape[1] // HEAD_DIM
    return jnp.concatenate([block[:, h * HEAD_DIM:(h + 1) * HEAD_DIM] for h in range(heads)], axis=0)


def pack_kernel(order, keys_ref, values_ref, out_ref, held, in_sems, out_sems):
    parts = out_ref.shape[0]
    loads = []
    for part in range(parts):
        for side, ref in enumerate((keys_ref, values_ref)):
            columns = ref.at[:, pl.ds(order[part] * HEAD_DIM, HEAD_DIM)]
            loads.append(pltpu.make_async_copy(columns, held.at[part, side], in_sems.at[part, side]))
            loads[-1].start()
    stores = []
    for part in range(parts):
        loads[2 * part].wait()
        loads[2 * part + 1].wait()
        stores.append(pltpu.make_async_copy(held.at[part], out_ref.at[part], out_sems.at[part]))
        stores[-1].start()
    for store in stores:
        store.wait()


def unpack_kernel(order, in_ref, keys_ref, values_ref, sems):
    copies = []
    for side, ref in enumerate((keys_ref, values_ref)):
        for part in range(in_ref.shape[0]):
            columns = ref.at[:, pl.ds(order[part] * HEAD_DIM, HEAD_DIM)]
            copies.append(pltpu.make_async_copy(in_ref.at[part, side], columns, sems.at[part, side]))
    for copy in copies:
        copy.start()
    for copy in copies:
        copy.wait()


def text_kernel(dp_ref, counts_ref, text_ref, q_ref, g_ref, flag_ref, qt_ref, gt_ref, q_out_ref, g_out_ref):
    found, position = owners(dp_ref[0], counts_ref, text_ref)
    mine = pick(found, position)
    for ref, out_ref, turned_ref in ((q_ref, q_out_ref, qt_ref), (g_ref, g_out_ref, gt_ref)):
        rows = head_rows(ref[mine])
        out_ref[...] = rows
        turned_ref[...] = rows.T
    for slot in range(GROUP):
        line = jnp.zeros((1, flag_ref.shape[1]), jnp.float32)
        flag_ref[slot:slot + 1] = line + jnp.where(found[slot] == mine, 1.0, 0.0)
        flag_ref[GROUP + slot:GROUP + slot + 1] = line + jnp.where(found[slot] == position, 1.0, 0.0)


def stats_kernel(order, qt_ref, gt_ref, kv_ref, stat_ref, weight_ref, grad_ref):
    parts, rows = kv_ref.shape[0], kv_ref.shape[2]
    q_turned, g_turned = qt_ref[...], gt_ref[...]
    wide = STEP * rows
    top = None
    for part in range(0, parts, STEP):
        block = kv_ref[part:part + STEP, 0].reshape(wide, HEAD_DIM)
        scores = jnp.dot(block, q_turned, preferred_element_type=jnp.float32) * SCALE2
        for place in range(part, part + STEP):
            dead = (order[place] + 1) * rows - TILE_ROWS
            if dead > 0:
                row = lax.broadcasted_iota(jnp.int32, scores.shape, 0) - (place - part) * rows
                scores = jnp.where((row >= max(rows - dead, 0)) & (row < rows), -1e30, scores)
        weight_ref[pl.ds(part * rows, wide), :] = scores
        part_top = jnp.max(scores, axis=0, keepdims=True)
        top = part_top if top is None else jnp.maximum(top, part_top)
    total = jnp.zeros_like(top)
    product = jnp.zeros_like(top)
    for part in range(0, parts, STEP):
        span = pl.ds(part * rows, wide)
        weights = jnp.exp2(weight_ref[span, :] - top)
        weight_ref[span, :] = weights
        block = kv_ref[part:part + STEP, 1].reshape(wide, HEAD_DIM)
        grads = jnp.dot(block, g_turned, preferred_element_type=jnp.float32)
        grad_ref[span, :] = grads
        total = total + jnp.sum(weights, axis=0, keepdims=True)
        product = product + jnp.sum(weights * grads, axis=0, keepdims=True)
    stat_ref[...] = jnp.concatenate([top, total, product, jnp.zeros((5, top.shape[1]), jnp.float32)], axis=0)


def merged(flag_ref, all_ref):
    tops = [jnp.where(flag_ref[slot:slot + 1] > 0, all_ref[slot][0:1], -1e30) for slot in range(GROUP)]
    top = functools.reduce(jnp.maximum, tops)
    total = jnp.zeros_like(top)
    product = jnp.zeros_like(top)
    for slot in range(GROUP):
        share = jnp.where(flag_ref[slot:slot + 1] > 0, jnp.exp2(tops[slot] - top), 0.0)
        total = total + share * all_ref[slot][1:2]
        product = product + share * all_ref[slot][2:3]
    return top, 1.0 / total, product / total


def grads_kernel(
    places, flag_ref, all_ref, own_ref, q_ref, g_ref, weight_ref, grad_ref, out_ref, dscore_ref, held, sems
):
    top, inverse, delta = merged(flag_ref, all_ref)
    rescale = jnp.exp2(own_ref[0:1] - top) * inverse
    parts, rows = out_ref.shape[0], out_ref.shape[2]
    q_rows, g_rows = q_ref[...], g_ref[...]
    copies = []
    for part in range(parts):
        span = pl.ds(part * rows, rows)
        probs = weight_ref[span, :] * rescale
        dscore = (probs * (grad_ref[span, :] - delta)).astype(jnp.bfloat16)
        dscore_ref[span, :] = dscore
        probs = probs.astype(jnp.bfloat16)
        place = places[part]
        held[place, 0] = (jnp.dot(dscore, q_rows, preferred_element_type=jnp.float32) * SCALE).astype(jnp.bfloat16)
        held[place, 1] = jnp.dot(probs, g_rows, preferred_element_type=jnp.float32).astype(jnp.bfloat16)
        copies.append(pltpu.make_async_copy(held.at[place], out_ref.at[place], sems.at[part]))
        copies[-1].start()
    for copy in copies:
        copy.wait()


def text_grad_kernel(kv_ref, dscore_ref, dq_ref):
    parts, rows = kv_ref.shape[0], kv_ref.shape[2]
    dq = None
    for part in range(parts):
        query_part = lax.dot_general(
            kv_ref[part, 0],
            dscore_ref[pl.ds(part * rows, rows), :],
            (((0,), (0,)), ((), ())),
            preferred_element_type=jnp.float32,
        )
        dq = query_part if dq is None else dq + query_part
    for head in range(dq.shape[1] // HEAD_DIM):
        cols = slice(head * HEAD_DIM, (head + 1) * HEAD_DIM)
        dq_ref[:, cols] = (dq[:, cols].T * SCALE).astype(jnp.bfloat16)


def query_kernel(flag_ref, parts_ref, out_ref):
    total = jnp.zeros(out_ref.shape, jnp.float32)
    for slot in range(GROUP):
        flag = flag_ref[GROUP + slot:GROUP + slot + 1]
        total = total + jnp.where(flag > 0, parts_ref[slot].astype(jnp.float32), 0.0)
    out_ref[...] = total.astype(jnp.bfloat16)


SMEM = pl.BlockSpec(memory_space=pltpu.SMEM)
VMEM = pl.BlockSpec(memory_space=pltpu.VMEM)
HBM = pl.BlockSpec(memory_space=pltpu.HBM)
ANY = pl.BlockSpec(memory_space=pl.ANY)
MIB = 1024 * 1024
STEP = 4


def call(kernel, out_shape, out_specs, in_specs, args, scratch=(), limit=32, flops=0, exps=0):
    outs = out_shape if isinstance(out_shape, tuple) else (out_shape,)
    moved = sum(a.size * a.dtype.itemsize for a in args) + sum(math.prod(o.shape) * 2 for o in outs)
    return pl.pallas_call(
        kernel,
        out_shape=out_shape,
        in_specs=in_specs,
        out_specs=out_specs,
        scratch_shapes=scratch,
        compiler_params=pltpu.CompilerParams(vmem_limit_bytes=limit * MIB),
        cost_estimate=pl.CostEstimate(flops=flops, bytes_accessed=moved, transcendentals=exps),
    )(*args)


def on_device(queries, keys, values, out_grad, tile_counts, text_sample):
    text_rows, width = queries.shape
    rows = keys.shape[0]
    parts = lax.axis_size("tensor")
    order = [7, 3, 2, 4, 1, 5, 0, 6]
    back_order = [5, 6, 7, 0, 1, 2, 3, 4]
    exchange = functools.partial(lax.all_to_all, axis_name="tensor", split_axis=0, concat_axis=0, tiled=True)
    devices = lax.axis_size("dp")
    groups = [[first + member for member in range(GROUP)] for first in range(0, devices, GROUP)]
    gather = functools.partial(lax.all_gather, axis_name="dp", axis_index_groups=groups)
    position = lax.axis_index("dp").astype(jnp.int32).reshape(1)
    heads = text_rows * width // HEAD_DIM
    matmul = 2 * heads * parts * rows * HEAD_DIM
    half = jnp.bfloat16
    full = jnp.float32
    blocks = (parts, 2, rows, HEAD_DIM)

    packed = call(
        functools.partial(pack_kernel, order),
        pltpu.HBM(blocks, half),
        HBM,
        [ANY, ANY],
        (keys, values),
        scratch=[
            pltpu.VMEM(blocks, half),
            pltpu.SemaphoreType.DMA((parts, 2)),
            pltpu.SemaphoreType.DMA((parts,)),
        ],
        limit=60,
    )
    kv = exchange(packed, axis_index_groups=[order])
    q_all = gather(queries)
    g_all = gather(out_grad)
    flags, q_turned, g_turned, q_rows, g_rows = call(
        text_kernel,
        (
            pltpu.VMEM((2 * GROUP, heads), full),
            pltpu.VMEM((HEAD_DIM, heads), half),
            pltpu.VMEM((HEAD_DIM, heads), half),
            pltpu.VMEM((heads, HEAD_DIM), half),
            pltpu.VMEM((heads, HEAD_DIM), half),
        ),
        (VMEM,) * 5,
        [SMEM] * 3 + [VMEM] * 2,
        (position, tile_counts, text_sample, q_all, g_all),
    )
    stats, weights, grad_prod = call(
        functools.partial(stats_kernel, order),
        (
            pltpu.VMEM((8, heads), full),
            pltpu.VMEM((parts * rows, heads), full),
            pltpu.VMEM((parts * rows, heads), full),
        ),
        (VMEM,) * 3,
        [VMEM] * 3,
        (q_turned, g_turned, kv),
        flops=2 * matmul,
        exps=heads * parts * rows,
    )
    stats_all = gather(stats)
    grads, dscore = call(
        functools.partial(grads_kernel, [back_order.index(member) for member in order]),
        (pltpu.HBM(blocks, half), pltpu.VMEM((parts * rows, heads), half)),
        (HBM, VMEM),
        [VMEM] * 7,
        (flags, stats_all, stats, q_rows, g_rows, weights, grad_prod),
        scratch=[pltpu.VMEM(blocks, half), pltpu.SemaphoreType.DMA((parts,))],
        flops=2 * matmul,
    )
    back = exchange(grads, axis_index_groups=[back_order])
    dq = call(
        text_grad_kernel,
        pltpu.VMEM((text_rows, width), half),
        VMEM,
        [VMEM] * 2,
        (kv, dscore),
        flops=matmul,
    )
    dq_all = gather(dq)
    query_grad = call(
        query_kernel, jax.ShapeDtypeStruct((text_rows, width), half), VMEM, [VMEM] * 2, (flags, dq_all)
    )
    tile = jax.ShapeDtypeStruct((rows, parts * HEAD_DIM), half)
    key_grad, value_grad = call(
        functools.partial(unpack_kernel, back_order),
        (tile, tile),
        (ANY, ANY),
        [ANY],
        (back,),
        scratch=[pltpu.SemaphoreType.DMA((parts, 2))],
        limit=8,
    )
    return query_grad, key_grad, value_grad


def solution(mesh):
    return jax.shard_map(
        on_device,
        mesh=mesh,
        in_specs=(
            P("dp", "tensor"),
            P(("dp", "tensor"), None),
            P(("dp", "tensor"), None),
            P("dp", "tensor"),
            P(),
            P(),
        ),
        out_specs=(P("dp", "tensor"), P(("dp", "tensor"), None), P(("dp", "tensor"), None)),
        check_vma=False,
    )
```

```python
import functools
import math

import jax
import jax.numpy as jnp
from jax import lax
from jax.experimental import pallas as pl
from jax.experimental.pallas import tpu as pltpu
from jax.sharding import PartitionSpec as P

HEAD_DIM = 128
TILE_ROWS = 1601
GROUP = 4
SCALE = HEAD_DIM ** -0.5
LOG2E = 1.4426950408889634
SCALE2 = SCALE * LOG2E


def owners(dp, counts, text):
    first = (dp // GROUP) * GROUP
    end0 = counts[first]
    end1 = end0 + counts[first + 1]
    end2 = end1 + counts[first + 2]
    found = []
    for slot in range(GROUP):
        sample = first
        for end in (end0, end1, end2):
            sample = sample + jnp.where(end <= slot, 1, 0)
        owner = jnp.int32(0)
        for member in range(1, GROUP):
            owner = owner + jnp.where(text[first + member] == sample, member, 0)
        found.append(owner)
    return found, dp - first


def pick(options, position):
    chosen = options[0]
    for index in range(1, GROUP):
        chosen = jnp.where(position == index, options[index], chosen)
    return chosen


def head_rows(block):
    heads = block.shape[1] // HEAD_DIM
    return jnp.concatenate([block[:, h * HEAD_DIM:(h + 1) * HEAD_DIM] for h in range(heads)], axis=0)


def pack_kernel(order, keys_ref, values_ref, out_ref, held, in_sems, out_sems):
    parts = out_ref.shape[0]
    loads = []
    for part in range(parts):
        for side, ref in enumerate((keys_ref, values_ref)):
            columns = ref.at[:, pl.ds(order[part] * HEAD_DIM, HEAD_DIM)]
            loads.append(pltpu.make_async_copy(columns, held.at[part, side], in_sems.at[part, side]))
            loads[-1].start()
    stores = []
    for part in range(parts):
        loads[2 * part].wait()
        loads[2 * part + 1].wait()
        stores.append(pltpu.make_async_copy(held.at[part], out_ref.at[part], out_sems.at[part]))
        stores[-1].start()
    for store in stores:
        store.wait()


def unpack_kernel(order, in_ref, keys_ref, values_ref, sems):
    copies = []
    for side, ref in enumerate((keys_ref, values_ref)):
        for part in range(in_ref.shape[0]):
            columns = ref.at[:, pl.ds(order[part] * HEAD_DIM, HEAD_DIM)]
            copies.append(pltpu.make_async_copy(in_ref.at[part, side], columns, sems.at[part, side]))
    for copy in copies:
        copy.start()
    for copy in copies:
        copy.wait()


def text_kernel(dp_ref, counts_ref, text_ref, q_ref, g_ref, flag_ref, qt_ref, gt_ref, q_out_ref, g_out_ref):
    found, position = owners(dp_ref[0], counts_ref, text_ref)
    mine = pick(found, position)
    for ref, out_ref, turned_ref in ((q_ref, q_out_ref, qt_ref), (g_ref, g_out_ref, gt_ref)):
        rows = head_rows(ref[mine])
        out_ref[...] = rows
        turned_ref[...] = rows.T
    for slot in range(GROUP):
        line = jnp.zeros((1, flag_ref.shape[1]), jnp.float32)
        flag_ref[slot:slot + 1] = line + jnp.where(found[slot] == mine, 1.0, 0.0)
        flag_ref[GROUP + slot:GROUP + slot + 1] = line + jnp.where(found[slot] == position, 1.0, 0.0)


def stats_kernel(order, qt_ref, gt_ref, kv_ref, stat_ref, weight_ref, grad_ref):
    parts, rows = kv_ref.shape[0], kv_ref.shape[2]
    q_turned, g_turned = qt_ref[...], gt_ref[...]
    top = None
    for part in range(parts):
        scores = jnp.dot(kv_ref[part, 0], q_turned, preferred_element_type=jnp.float32) * SCALE2
        if (order[part] + 1) * rows > TILE_ROWS:
            row = lax.broadcasted_iota(jnp.int32, scores.shape, 0) + order[part] * rows
            scores = jnp.where(row < TILE_ROWS, scores, -1e30)
        weight_ref[pl.ds(part * rows, rows), :] = scores
        part_top = jnp.max(scores, axis=0, keepdims=True)
        top = part_top if top is None else jnp.maximum(top, part_top)
    total = jnp.zeros_like(top)
    product = jnp.zeros_like(top)
    for part in range(parts):
        span = pl.ds(part * rows, rows)
        weights = jnp.exp2(weight_ref[span, :] - top)
        weight_ref[span, :] = weights
        grads = jnp.dot(kv_ref[part, 1], g_turned, preferred_element_type=jnp.float32)
        grad_ref[span, :] = grads
        total = total + jnp.sum(weights, axis=0, keepdims=True)
        product = product + jnp.sum(weights * grads, axis=0, keepdims=True)
    stat_ref[...] = jnp.concatenate([top, total, product, jnp.zeros((5, top.shape[1]), jnp.float32)], axis=0)


def merged(flag_ref, all_ref):
    tops = [jnp.where(flag_ref[slot:slot + 1] > 0, all_ref[slot][0:1], -1e30) for slot in range(GROUP)]
    top = functools.reduce(jnp.maximum, tops)
    total = jnp.zeros_like(top)
    product = jnp.zeros_like(top)
    for slot in range(GROUP):
        share = jnp.where(flag_ref[slot:slot + 1] > 0, jnp.exp2(tops[slot] - top), 0.0)
        total = total + share * all_ref[slot][1:2]
        product = product + share * all_ref[slot][2:3]
    return top, 1.0 / total, product / total


def grads_kernel(
    places, flag_ref, all_ref, own_ref, q_ref, g_ref, weight_ref, grad_ref, out_ref, dscore_ref, held, sems
):
    top, inverse, delta = merged(flag_ref, all_ref)
    rescale = jnp.exp2(own_ref[0:1] - top) * inverse
    parts, rows = out_ref.shape[0], out_ref.shape[2]
    q_rows, g_rows = q_ref[...], g_ref[...]
    copies = []
    for part in range(parts):
        span = pl.ds(part * rows, rows)
        probs = weight_ref[span, :] * rescale
        dscore = (probs * (grad_ref[span, :] - delta)).astype(jnp.bfloat16)
        dscore_ref[span, :] = dscore
        probs = probs.astype(jnp.bfloat16)
        place = places[part]
        held[place, 0] = (jnp.dot(dscore, q_rows, preferred_element_type=jnp.float32) * SCALE).astype(jnp.bfloat16)
        held[place, 1] = jnp.dot(probs, g_rows, preferred_element_type=jnp.float32).astype(jnp.bfloat16)
        copies.append(pltpu.make_async_copy(held.at[place], out_ref.at[place], sems.at[part]))
        copies[-1].start()
    for copy in copies:
        copy.wait()


def text_grad_kernel(kv_ref, dscore_ref, dq_ref):
    parts, rows = kv_ref.shape[0], kv_ref.shape[2]
    dq = None
    for part in range(parts):
        query_part = lax.dot_general(
            kv_ref[part, 0],
            dscore_ref[pl.ds(part * rows, rows), :],
            (((0,), (0,)), ((), ())),
            preferred_element_type=jnp.float32,
        )
        dq = query_part if dq is None else dq + query_part
    for head in range(dq.shape[1] // HEAD_DIM):
        cols = slice(head * HEAD_DIM, (head + 1) * HEAD_DIM)
        dq_ref[:, cols] = (dq[:, cols].T * SCALE).astype(jnp.bfloat16)


def query_kernel(flag_ref, parts_ref, out_ref):
    total = jnp.zeros(out_ref.shape, jnp.float32)
    for slot in range(GROUP):
        flag = flag_ref[GROUP + slot:GROUP + slot + 1]
        total = total + jnp.where(flag > 0, parts_ref[slot].astype(jnp.float32), 0.0)
    out_ref[...] = total.astype(jnp.bfloat16)


SMEM = pl.BlockSpec(memory_space=pltpu.SMEM)
VMEM = pl.BlockSpec(memory_space=pltpu.VMEM)
HBM = pl.BlockSpec(memory_space=pltpu.HBM)
ANY = pl.BlockSpec(memory_space=pl.ANY)
MIB = 1024 * 1024


def call(kernel, out_shape, out_specs, in_specs, args, scratch=(), limit=32, flops=0, exps=0):
    outs = out_shape if isinstance(out_shape, tuple) else (out_shape,)
    moved = sum(a.size * a.dtype.itemsize for a in args) + sum(math.prod(o.shape) * 2 for o in outs)
    return pl.pallas_call(
        kernel,
        out_shape=out_shape,
        in_specs=in_specs,
        out_specs=out_specs,
        scratch_shapes=scratch,
        compiler_params=pltpu.CompilerParams(vmem_limit_bytes=limit * MIB),
        cost_estimate=pl.CostEstimate(flops=flops, bytes_accessed=moved, transcendentals=exps),
    )(*args)


def on_device(queries, keys, values, out_grad, tile_counts, text_sample):
    text_rows, width = queries.shape
    rows = keys.shape[0]
    parts = lax.axis_size("tensor")
    order = [7, 3, 2, 4, 1, 5, 0, 6]
    back_order = [5, 6, 7, 0, 1, 2, 3, 4]
    exchange = functools.partial(lax.all_to_all, axis_name="tensor", split_axis=0, concat_axis=0, tiled=True)
    devices = lax.axis_size("dp")
    groups = [[first + member for member in range(GROUP)] for first in range(0, devices, GROUP)]
    gather = functools.partial(lax.all_gather, axis_name="dp", axis_index_groups=groups)
    position = lax.axis_index("dp").astype(jnp.int32).reshape(1)
    heads = text_rows * width // HEAD_DIM
    matmul = 2 * heads * parts * rows * HEAD_DIM
    half = jnp.bfloat16
    full = jnp.float32
    blocks = (parts, 2, rows, HEAD_DIM)

    packed = call(
        functools.partial(pack_kernel, order),
        pltpu.HBM(blocks, half),
        HBM,
        [ANY, ANY],
        (keys, values),
        scratch=[
            pltpu.VMEM(blocks, half),
            pltpu.SemaphoreType.DMA((parts, 2)),
            pltpu.SemaphoreType.DMA((parts,)),
        ],
        limit=60,
    )
    kv = exchange(packed, axis_index_groups=[order])
    q_all = gather(queries)
    g_all = gather(out_grad)
    flags, q_turned, g_turned, q_rows, g_rows = call(
        text_kernel,
        (
            pltpu.VMEM((2 * GROUP, heads), full),
            pltpu.VMEM((HEAD_DIM, heads), half),
            pltpu.VMEM((HEAD_DIM, heads), half),
            pltpu.VMEM((heads, HEAD_DIM), half),
            pltpu.VMEM((heads, HEAD_DIM), half),
        ),
        (VMEM,) * 5,
        [SMEM] * 3 + [VMEM] * 2,
        (position, tile_counts, text_sample, q_all, g_all),
    )
    stats, weights, grad_prod = call(
        functools.partial(stats_kernel, order),
        (
            pltpu.VMEM((8, heads), full),
            pltpu.VMEM((parts * rows, heads), full),
            pltpu.VMEM((parts * rows, heads), full),
        ),
        (VMEM,) * 3,
        [VMEM] * 3,
        (q_turned, g_turned, kv),
        flops=2 * matmul,
        exps=heads * parts * rows,
    )
    stats_all = gather(stats)
    grads, dscore = call(
        functools.partial(grads_kernel, [back_order.index(member) for member in order]),
        (pltpu.HBM(blocks, half), pltpu.VMEM((parts * rows, heads), half)),
        (HBM, VMEM),
        [VMEM] * 7,
        (flags, stats_all, stats, q_rows, g_rows, weights, grad_prod),
        scratch=[pltpu.VMEM(blocks, half), pltpu.SemaphoreType.DMA((parts,))],
        flops=2 * matmul,
    )
    back = exchange(grads, axis_index_groups=[back_order])
    dq = call(
        text_grad_kernel,
        pltpu.VMEM((text_rows, width), half),
        VMEM,
        [VMEM] * 2,
        (kv, dscore),
        flops=matmul,
    )
    dq_all = gather(dq)
    query_grad = call(
        query_kernel, jax.ShapeDtypeStruct((text_rows, width), half), VMEM, [VMEM] * 2, (flags, dq_all)
    )
    tile = jax.ShapeDtypeStruct((rows, parts * HEAD_DIM), half)
    key_grad, value_grad = call(
        functools.partial(unpack_kernel, back_order),
        (tile, tile),
        (ANY, ANY),
        [ANY],
        (back,),
        scratch=[pltpu.SemaphoreType.DMA((parts, 2))],
        limit=8,
    )
    return query_grad, key_grad, value_grad


def solution(mesh):
    return jax.shard_map(
        on_device,
        mesh=mesh,
        in_specs=(
            P("dp", "tensor"),
            P(("dp", "tensor"), None),
            P(("dp", "tensor"), None),
            P("dp", "tensor"),
            P(),
            P(),
        ),
        out_specs=(P("dp", "tensor"), P(("dp", "tensor"), None), P(("dp", "tensor"), None)),
        check_vma=False,
    )
```

```python
import functools
import math

import jax
import jax.numpy as jnp
from jax import lax
from jax.experimental import pallas as pl
from jax.experimental.pallas import tpu as pltpu
from jax.sharding import PartitionSpec as P

HEAD_DIM = 128
TILE_ROWS = 1601
GROUP = 4
SCALE = HEAD_DIM ** -0.5
LOG2E = 1.4426950408889634
SCALE2 = SCALE * LOG2E


def owners(dp, counts, text):
    first = (dp // GROUP) * GROUP
    end0 = counts[first]
    end1 = end0 + counts[first + 1]
    end2 = end1 + counts[first + 2]
    found = []
    for slot in range(GROUP):
        sample = first
        for end in (end0, end1, end2):
            sample = sample + jnp.where(end <= slot, 1, 0)
        owner = jnp.int32(0)
        for member in range(1, GROUP):
            owner = owner + jnp.where(text[first + member] == sample, member, 0)
        found.append(owner)
    return found, dp - first


def pick(options, position):
    chosen = options[0]
    for index in range(1, GROUP):
        chosen = jnp.where(position == index, options[index], chosen)
    return chosen


def head_rows(block):
    heads = block.shape[1] // HEAD_DIM
    return jnp.concatenate([block[:, h * HEAD_DIM:(h + 1) * HEAD_DIM] for h in range(heads)], axis=0)


def member_orders(size):
    return ([7, 1, 3, 5, 6, 0, 2, 4], [7, 0, 1, 2, 3, 4, 5, 6])


def column(orders, part):
    core = lax.axis_index("dp") % 2
    return pl.multiple_of(jnp.where(core == 0, orders[0][part], orders[1][part]) * HEAD_DIM, HEAD_DIM)


def pack_kernel(order, keys_ref, values_ref, out_ref, held, in_sems, out_sems):
    parts = out_ref.shape[0]
    loads = []
    for part in range(parts):
        for side, ref in enumerate((keys_ref, values_ref)):
            columns = ref.at[:, pl.ds(column(order, part), HEAD_DIM)]
            loads.append(pltpu.make_async_copy(columns, held.at[part, side], in_sems.at[part, side]))
            loads[-1].start()
    stores = []
    for part in range(parts):
        loads[2 * part].wait()
        loads[2 * part + 1].wait()
        stores.append(pltpu.make_async_copy(held.at[part], out_ref.at[part], out_sems.at[part]))
        stores[-1].start()
    for store in stores:
        store.wait()


def unpack_kernel(order, in_ref, keys_ref, values_ref, sems):
    copies = []
    for side, ref in enumerate((keys_ref, values_ref)):
        for part in range(in_ref.shape[0]):
            columns = ref.at[:, pl.ds(column(order, part), HEAD_DIM)]
            copies.append(pltpu.make_async_copy(in_ref.at[part, side], columns, sems.at[part, side]))
    for copy in copies:
        copy.start()
    for copy in copies:
        copy.wait()


def text_kernel(dp_ref, counts_ref, text_ref, q_ref, g_ref, flag_ref, qt_ref, gt_ref, q_out_ref, g_out_ref):
    found, position = owners(dp_ref[0], counts_ref, text_ref)
    mine = pick(found, position)
    for ref, out_ref, turned_ref in ((q_ref, q_out_ref, qt_ref), (g_ref, g_out_ref, gt_ref)):
        rows = head_rows(ref[mine])
        out_ref[...] = rows
        turned_ref[...] = rows.T
    for slot in range(GROUP):
        line = jnp.zeros((1, flag_ref.shape[1]), jnp.float32)
        flag_ref[slot:slot + 1] = line + jnp.where(found[slot] == mine, 1.0, 0.0)
        flag_ref[GROUP + slot:GROUP + slot + 1] = line + jnp.where(found[slot] == position, 1.0, 0.0)


def stats_kernel(order, qt_ref, gt_ref, kv_ref, stat_ref, weight_ref, grad_ref):
    parts, rows = kv_ref.shape[0], kv_ref.shape[2]
    q_turned, g_turned = qt_ref[...], gt_ref[...]
    top = None
    for part in range(parts):
        scores = jnp.dot(kv_ref[part, 0], q_turned, preferred_element_type=jnp.float32) * SCALE2
        if (order[part] + 1) * rows > TILE_ROWS:
            row = lax.broadcasted_iota(jnp.int32, scores.shape, 0) + order[part] * rows
            scores = jnp.where(row < TILE_ROWS, scores, -1e30)
        weight_ref[pl.ds(part * rows, rows), :] = scores
        part_top = jnp.max(scores, axis=0, keepdims=True)
        top = part_top if top is None else jnp.maximum(top, part_top)
    total = jnp.zeros_like(top)
    product = jnp.zeros_like(top)
    for part in range(parts):
        span = pl.ds(part * rows, rows)
        weights = jnp.exp2(weight_ref[span, :] - top)
        weight_ref[span, :] = weights
        grads = jnp.dot(kv_ref[part, 1], g_turned, preferred_element_type=jnp.float32)
        grad_ref[span, :] = grads
        total = total + jnp.sum(weights, axis=0, keepdims=True)
        product = product + jnp.sum(weights * grads, axis=0, keepdims=True)
    stat_ref[...] = jnp.concatenate([top, total, product, jnp.zeros((5, top.shape[1]), jnp.float32)], axis=0)


def merged(flag_ref, all_ref):
    tops = [jnp.where(flag_ref[slot:slot + 1] > 0, all_ref[slot][0:1], -1e30) for slot in range(GROUP)]
    top = functools.reduce(jnp.maximum, tops)
    total = jnp.zeros_like(top)
    product = jnp.zeros_like(top)
    for slot in range(GROUP):
        share = jnp.where(flag_ref[slot:slot + 1] > 0, jnp.exp2(tops[slot] - top), 0.0)
        total = total + share * all_ref[slot][1:2]
        product = product + share * all_ref[slot][2:3]
    return top, 1.0 / total, product / total


def grads_kernel(
    places, flag_ref, all_ref, own_ref, q_ref, g_ref, weight_ref, grad_ref, out_ref, dscore_ref, held, sems
):
    top, inverse, delta = merged(flag_ref, all_ref)
    rescale = jnp.exp2(own_ref[0:1] - top) * inverse
    parts, rows = out_ref.shape[0], out_ref.shape[2]
    q_rows, g_rows = q_ref[...], g_ref[...]
    copies = []
    for part in range(parts):
        span = pl.ds(part * rows, rows)
        probs = weight_ref[span, :] * rescale
        dscore = (probs * (grad_ref[span, :] - delta)).astype(jnp.bfloat16)
        dscore_ref[span, :] = dscore
        probs = probs.astype(jnp.bfloat16)
        place = places[part]
        held[place, 0] = (jnp.dot(dscore, q_rows, preferred_element_type=jnp.float32) * SCALE).astype(jnp.bfloat16)
        held[place, 1] = jnp.dot(probs, g_rows, preferred_element_type=jnp.float32).astype(jnp.bfloat16)
        copies.append(pltpu.make_async_copy(held.at[place], out_ref.at[place], sems.at[part]))
        copies[-1].start()
    for copy in copies:
        copy.wait()


def text_grad_kernel(kv_ref, dscore_ref, dq_ref):
    parts, rows = kv_ref.shape[0], kv_ref.shape[2]
    dq = None
    for part in range(parts):
        query_part = lax.dot_general(
            kv_ref[part, 0],
            dscore_ref[pl.ds(part * rows, rows), :],
            (((0,), (0,)), ((), ())),
            preferred_element_type=jnp.float32,
        )
        dq = query_part if dq is None else dq + query_part
    for head in range(dq.shape[1] // HEAD_DIM):
        cols = slice(head * HEAD_DIM, (head + 1) * HEAD_DIM)
        dq_ref[:, cols] = (dq[:, cols].T * SCALE).astype(jnp.bfloat16)


def query_kernel(flag_ref, parts_ref, out_ref):
    total = jnp.zeros(out_ref.shape, jnp.float32)
    for slot in range(GROUP):
        flag = flag_ref[GROUP + slot:GROUP + slot + 1]
        total = total + jnp.where(flag > 0, parts_ref[slot].astype(jnp.float32), 0.0)
    out_ref[...] = total.astype(jnp.bfloat16)


SMEM = pl.BlockSpec(memory_space=pltpu.SMEM)
VMEM = pl.BlockSpec(memory_space=pltpu.VMEM)
HBM = pl.BlockSpec(memory_space=pltpu.HBM)
ANY = pl.BlockSpec(memory_space=pl.ANY)
MIB = 1024 * 1024


def call(kernel, out_shape, out_specs, in_specs, args, scratch=(), limit=32, flops=0, exps=0):
    outs = out_shape if isinstance(out_shape, tuple) else (out_shape,)
    moved = sum(a.size * a.dtype.itemsize for a in args) + sum(math.prod(o.shape) * 2 for o in outs)
    return pl.pallas_call(
        kernel,
        out_shape=out_shape,
        in_specs=in_specs,
        out_specs=out_specs,
        scratch_shapes=scratch,
        compiler_params=pltpu.CompilerParams(vmem_limit_bytes=limit * MIB),
        cost_estimate=pl.CostEstimate(flops=flops, bytes_accessed=moved, transcendentals=exps),
    )(*args)


def on_device(queries, keys, values, out_grad, tile_counts, text_sample):
    text_rows, width = queries.shape
    rows = keys.shape[0]
    parts = lax.axis_size("tensor")
    devices = lax.axis_size("dp")
    orders = member_orders(parts)
    members = [[dp * parts + member for member in orders[dp % 2]] for dp in range(devices)]
    exchange = functools.partial(
        lax.all_to_all,
        axis_name=("dp", "tensor"),
        split_axis=0,
        concat_axis=0,
        axis_index_groups=members,
        tiled=True,
    )
    groups = [[first + member for member in range(GROUP)] for first in range(0, devices, GROUP)]
    gather = functools.partial(lax.all_gather, axis_name="dp", axis_index_groups=groups)
    position = lax.axis_index("dp").astype(jnp.int32).reshape(1)
    heads = text_rows * width // HEAD_DIM
    matmul = 2 * heads * parts * rows * HEAD_DIM
    half = jnp.bfloat16
    full = jnp.float32
    blocks = (parts, 2, rows, HEAD_DIM)

    packed = call(
        functools.partial(pack_kernel, orders),
        pltpu.HBM(blocks, half),
        HBM,
        [ANY, ANY],
        (keys, values),
        scratch=[
            pltpu.VMEM(blocks, half),
            pltpu.SemaphoreType.DMA((parts, 2)),
            pltpu.SemaphoreType.DMA((parts,)),
        ],
        limit=60,
    )
    kv = exchange(packed)
    q_all = gather(queries)
    g_all = gather(out_grad)
    flags, q_turned, g_turned, q_rows, g_rows = call(
        text_kernel,
        (
            pltpu.VMEM((2 * GROUP, heads), full),
            pltpu.VMEM((HEAD_DIM, heads), half),
            pltpu.VMEM((HEAD_DIM, heads), half),
            pltpu.VMEM((heads, HEAD_DIM), half),
            pltpu.VMEM((heads, HEAD_DIM), half),
        ),
        (VMEM,) * 5,
        [SMEM] * 3 + [VMEM] * 2,
        (position, tile_counts, text_sample, q_all, g_all),
    )
    stats, weights, grad_prod = call(
        functools.partial(stats_kernel, orders[0]),
        (
            pltpu.VMEM((8, heads), full),
            pltpu.VMEM((parts * rows, heads), full),
            pltpu.VMEM((parts * rows, heads), full),
        ),
        (VMEM,) * 3,
        [VMEM] * 3,
        (q_turned, g_turned, kv),
        flops=2 * matmul,
        exps=heads * parts * rows,
    )
    stats_all = gather(stats)
    grads, dscore = call(
        functools.partial(grads_kernel, list(range(parts))),
        (pltpu.HBM(blocks, half), pltpu.VMEM((parts * rows, heads), half)),
        (HBM, VMEM),
        [VMEM] * 7,
        (flags, stats_all, stats, q_rows, g_rows, weights, grad_prod),
        scratch=[pltpu.VMEM(blocks, half), pltpu.SemaphoreType.DMA((parts,))],
        flops=2 * matmul,
    )
    back = exchange(grads)
    dq = call(
        text_grad_kernel,
        pltpu.VMEM((text_rows, width), half),
        VMEM,
        [VMEM] * 2,
        (kv, dscore),
        flops=matmul,
    )
    dq_all = gather(dq)
    query_grad = call(
        query_kernel, jax.ShapeDtypeStruct((text_rows, width), half), VMEM, [VMEM] * 2, (flags, dq_all)
    )
    tile = jax.ShapeDtypeStruct((rows, parts * HEAD_DIM), half)
    key_grad, value_grad = call(
        functools.partial(unpack_kernel, orders),
        (tile, tile),
        (ANY, ANY),
        [ANY],
        (back,),
        scratch=[pltpu.SemaphoreType.DMA((parts, 2))],
        limit=8,
    )
    return query_grad, key_grad, value_grad


def solution(mesh):
    return jax.shard_map(
        on_device,
        mesh=mesh,
        in_specs=(
            P("dp", "tensor"),
            P(("dp", "tensor"), None),
            P(("dp", "tensor"), None),
            P("dp", "tensor"),
            P(),
            P(),
        ),
        out_specs=(P("dp", "tensor"), P(("dp", "tensor"), None), P(("dp", "tensor"), None)),
        check_vma=False,
    )
```
